32 devices in a mesh: section: 8 (over z, y), fsdp: 4 (over x, core).
Axes of the slice: x: 2, y: 2, z: 4, core: 2. Of those that a mesh axis runs over, the one named last changes fastest.
Arguments:
- branch_in: bfloat16 [8, 8192, 128], P('section', 'fsdp'), may hold values from -0.0625 to 0.0625
- branch_out: bfloat16 [8, 128, 8192], P('section', None, 'fsdp'), may hold values from -0.5 to 0.5
- down_inputs: bfloat16 [8, 12, 32, 8192], P('section', None, 'fsdp'), may hold values from -6 to 6
- up_inputs: bfloat16 [8, 12, 32, 8192], P('section', None, 'fsdp'), may hold values from -6 to 6
- top_grads: bfloat16 [2, 12, 32, 8192], P(None, None, 'fsdp'), may hold values from -6 to 6
- plan: int32 [2, 12], replicated, may hold values from 0 to 11, each once within a row
- reward_pos: int32 [2, 12, 4], replicated, may hold values from 0 to 7
- reward_cot: float32 [2, 12, 4], replicated, may hold values from -4 to 4
- reward_head: float32 [8192], replicated, may hold values from -5 to 5
Outputs:
- grad_in: float32 [8, 8192, 128], P('section', 'fsdp')
- grad_out: float32 [8, 128, 8192], P('section', None, 'fsdp')
The draws below stay inside these ranges and needn't reach their ends.
Inputs may be any that keep to these rules, and one draw needn't show every extreme that they name: Each row of plan names every microbatch once.
All inputs are finite; a program needn't handle non-finite values.
Results may differ from the reference program's by a relative error of at most 0.03.
Values may be sent and summed in bfloat16 or wider, within the bound.
A program may use at most 128 MiB of HBM per device.

```python
import jax
import jax.numpy as jnp
from jax import lax

D = 8192
R = 128
ROWS = 8
MICRO = 12
SEQS = 4
LAYERS = 8
TOK = 32
SEQ_LEN = 8
N_FSDP = 4


def touch_ends(drawn, own_key, smallest, largest):
    spot = [jax.random.randint(jax.random.fold_in(own_key, axis), (), 0, length) for axis, length in enumerate(drawn.shape)]
    widest = drawn.shape.index(max(drawn.shape))
    neighbour = spot[:widest] + [(spot[widest] + 1) % drawn.shape[widest]] + spot[widest + 1:]
    return drawn.at[tuple(spot)].set(smallest).at[tuple(neighbour)].set(largest)


def levels(stream_key, shape, shards, low, high):
    gain = 1.0
    for axis_at, shards_of in shards:
        steps = jax.random.uniform(jax.random.fold_in(jax.random.fold_in(stream_key, 6), axis_at), (shards_of,), jnp.float32, low / len(shards), high / len(shards))
        gain = gain * jnp.repeat(jnp.exp(steps), shape[axis_at] // shards_of).reshape((-1,) + (1,) * (len(shape) - 1 - axis_at))
    return gain


def centred(own_key, shape, width, limit, split=(), kind=jnp.bfloat16):
    drawn = jax.random.normal(own_key, shape, jnp.float32) * width
    if len(split) > 0:
        drawn = levels(own_key, shape, split, -0.22, 0.18) * drawn
    return jnp.clip(drawn, min=-limit, max=limit).astype(kind)


def setup_inputs(seed: int = 0) -> dict:
    keys = jax.random.split(jax.random.key(seed), 10)
    branch_in = centred(keys[0], (LAYERS, D, R), D ** -0.5, 0.0625, ((0, 8), (1, 4)))
    branch_out = centred(keys[1], (LAYERS, R, D), R ** -0.5, 0.5, ((0, 8), (2, 4)))
    down_inputs = centred(keys[2], (LAYERS, MICRO, TOK, D), 1.0, 6.0, ((0, 8), (2, 4)))
    up_inputs = centred(keys[3], (LAYERS, MICRO, TOK, D), 1.0, 6.0, ((0, 8), (2, 4)))
    top_grads = centred(keys[4], (2, MICRO, TOK, D), 1.0, 6.0, ((2, 4),))
    plan = jax.vmap(lambda own: jax.random.permutation(own, MICRO))(jax.random.split(keys[5], 2)).reshape((2, MICRO)).astype(jnp.int32)
    reward_pos = touch_ends(jax.random.randint(keys[6], (2, MICRO, SEQS), 0, SEQ_LEN), jax.random.fold_in(keys[6], 1), 0, SEQ_LEN - 1).astype(jnp.int32)
    reward_cot = centred(keys[7], (2, MICRO, SEQS), 1.0, 4.0, (), jnp.float32)
    reward_head = centred(keys[8], (D,), 1.0, 5.0, (), jnp.float32)
    return {"branch_in": branch_in, "branch_out": branch_out, "down_inputs": down_inputs, "up_inputs": up_inputs, "top_grads": top_grads, "plan": plan, "reward_pos": reward_pos, "reward_cot": reward_cot, "reward_head": reward_head}


def branch_grads(inputs, grad, w_in, w_out):
    pre_act = jnp.dot(inputs, w_in, preferred_element_type=jnp.float32)
    sig_val = jax.nn.sigmoid(pre_act)
    hidden = (pre_act * sig_val).astype(jnp.bfloat16)
    grad_hidden = lax.dot_general(grad, w_out, (((1,), (1,)), ((), ())), preferred_element_type=jnp.float32)
    grad_pre = (grad_hidden * sig_val * (1.0 + pre_act * (1.0 - sig_val))).astype(jnp.bfloat16)
    back_term = lax.dot_general(grad_pre, w_in, (((1,), (1,)), ((), ())), preferred_element_type=jnp.float32)
    back = (grad.astype(jnp.float32) + back_term).astype(jnp.bfloat16)
    return hidden, grad_pre, back


def block_sums(inputs, hidden, grad, grad_pre):
    in_blocks = inputs.reshape(MICRO, N_FSDP, ROWS, D).astype(jnp.float32)
    hid_blocks = hidden.reshape(MICRO, N_FSDP, ROWS, R).astype(jnp.float32)
    grad_blocks = grad.reshape(MICRO, N_FSDP, ROWS, D).astype(jnp.float32)
    pre_blocks = grad_pre.reshape(MICRO, N_FSDP, ROWS, R).astype(jnp.float32)
    part_in = jnp.einsum('mfrd,mfrk->fdk', in_blocks, pre_blocks)
    part_out = jnp.einsum('mfrk,mfrd->fkd', hid_blocks, grad_blocks)
    part_in = part_in.astype(jnp.bfloat16).astype(jnp.float32)
    part_out = part_out.astype(jnp.bfloat16).astype(jnp.float32)
    return jnp.sum(part_in, axis=0), jnp.sum(part_out, axis=0)


def layer_step(grad, pieces):
    inputs, w_in, w_out = pieces
    flat_in = inputs.reshape(MICRO * TOK, D)
    flat_grad = grad.reshape(MICRO * TOK, D)
    hidden, grad_pre, back = branch_grads(flat_in, flat_grad, w_in, w_out)
    part_in, part_out = block_sums(flat_in, hidden, flat_grad, grad_pre)
    back = back.reshape(MICRO, TOK, D)
    return back, (part_in, part_out)


def first_gradient(top, order, positions, rewards, head):
    placed = jnp.zeros_like(top).at[order].set(top)
    target = jnp.arange(SEQS, dtype=jnp.int32)[None, :] * SEQ_LEN + positions
    match = target[:, :, None] == jnp.arange(TOK, dtype=jnp.int32)[None, None, :]
    row_weight = jnp.sum(jnp.where(match, rewards[:, :, None], jnp.zeros((), jnp.float32)), axis=1)
    total = placed.astype(jnp.float32) + row_weight[:, :, None] * head[None, None, :]
    return total.astype(jnp.bfloat16)


def reference(branch_in, branch_out, down_inputs, up_inputs, top_grads, plan, reward_pos, reward_cot, reward_head):
    first_down = first_gradient(top_grads[0], plan[0], reward_pos[0], reward_cot[0], reward_head)
    first_up = first_gradient(top_grads[1], plan[1], reward_pos[1], reward_cot[1], reward_head)
    _, (down_in, down_out) = lax.scan(layer_step, first_down, (down_inputs[::-1], branch_in[::-1], branch_out[::-1]))
    _, (up_in, up_out) = lax.scan(layer_step, first_up, (up_inputs, branch_in[::-1], branch_out[::-1]))
    grad_in = down_in[::-1] + up_in[::-1]
    grad_out = down_out[::-1] + up_out[::-1]
    return grad_in, grad_out
```

```python
import jax
import jax.numpy as jnp
from jax import lax
from jax.sharding import PartitionSpec as P

BF = jnp.bfloat16
F32 = jnp.float32


def dot(a, b, ca, cb):
    return lax.dot_general(a, b, (((ca,), (cb,)), ((), ())), preferred_element_type=F32)


def on_device(
    branch_in,
    branch_out,
    down_inputs,
    up_inputs,
    top_grads,
    plan,
    reward_pos,
    reward_cot,
    reward_head,
):
    S = lax.axis_size("section")
    k = lax.axis_index("section")
    F = lax.axis_size("fsdp")
    f = lax.axis_index("fsdp")
    _, micro, r, D = down_inputs.shape
    n = micro * r
    seqs = reward_pos.shape[2]
    seq_len = r * F // seqs
    w_in, w_out = branch_in[0], branch_out[0]
    R = w_in.shape[1]

    x = jnp.stack([down_inputs[0].reshape(n, D), up_inputs[0].reshape(n, D)])
    xs = lax.all_to_all(x, "fsdp", split_axis=2, concat_axis=1, tiled=True)
    w_all = lax.all_gather(w_in, "section", axis=0, tiled=False)

    row_global = f * r + jnp.arange(r, dtype=jnp.int32)
    pick = plan[:, :, None] == jnp.arange(micro, dtype=jnp.int32)
    reward_pos = jnp.sum(jnp.where(pick[..., None], reward_pos[:, None], 0), axis=2)
    reward_cot = jnp.sum(jnp.where(pick[..., None], reward_cot[:, None], 0.0), axis=2)
    order = jnp.einsum(
        "djm,rs->djrms", pick.astype(BF), jnp.eye(r, dtype=BF), preferred_element_type=F32
    )
    order = order.astype(BF).reshape(2, n, n)
    target = jnp.arange(seqs, dtype=jnp.int32) * seq_len + reward_pos
    weight = jnp.sum(
        jnp.where(target[..., None] == row_global, reward_cot[..., None], 0.0), axis=2
    )
    first = (top_grads.astype(F32) + weight[..., None] * reward_head).astype(BF)
    gs = lax.all_to_all(
        first.reshape(2, n, D), "fsdp", split_axis=2, concat_axis=1, tiled=True
    )
    N = n * F

    w_far = lax.dynamic_index_in_dim(w_all, S - 1 - k, 0, keepdims=False)
    pre = [dot(xs[0], w_in, 1, 0), dot(xs[1], w_far, 1, 0)]
    top = dot(gs.reshape(2 * N, -1), w_out, 1, 1).reshape(2, N, R)
    parts = jnp.stack([pre[0], pre[1], top[0], top[1]]).astype(BF)
    mix = lax.dot_general(
        w_all, w_out, (((1,), (1,)), ((), ())), preferred_element_type=F32
    ).astype(BF)
    parts = lax.psum_scatter(parts, "fsdp", scatter_dimension=1, tiled=True)
    mix = lax.psum_scatter(mix, "fsdp", scatter_dimension=1, tiled=True)
    parts = lax.all_gather(parts, "section", axis=0)
    mix = lax.all_gather(mix, ("section", "fsdp"), axis=0)
    mix = mix.reshape(S, F, S, R // F, R).transpose(0, 2, 1, 3, 4).reshape(S, S, R, R)

    pres = jnp.einsum("dij,ldjr->ldir", order, parts[:, :2], preferred_element_type=F32)

    grads = [None] * S
    hiddens = [None] * S
    for l in range(S - 1, -1, -1):
        p = jnp.concatenate([pres[l, 0], pres[S - 1 - l, 1]])
        gh = parts[l, 2:4].reshape(2 * n, R).astype(F32)
        if l < S - 1:
            above = jnp.concatenate(grads[l + 1 :], axis=1)
            gh = gh + dot(above, mix[l, l + 1 :].reshape(-1, R), 1, 0)
        sig = jax.nn.sigmoid(p)
        hiddens[l] = (p * sig).astype(BF)
        grads[l] = (gh * sig * (1.0 + p * (1.0 - sig))).astype(BF)
    gp = jnp.stack(grads)
    hid = lax.dynamic_index_in_dim(jnp.stack(hiddens), k, 0, keepdims=False)
    gp_dn = lax.dynamic_index_in_dim(gp, k, 0, keepdims=False)[:n]
    gp_up = lax.dynamic_index_in_dim(gp, S - 1 - k, 0, keepdims=False)[n:]
    gp_dn = dot(order[0], gp_dn, 0, 0).astype(BF)
    gp_up = dot(order[1], gp_up, 0, 0).astype(BF)
    small = jnp.stack([gp_dn, gp_up, hid[:n], hid[n:]])
    small = lax.all_gather(small, "fsdp", axis=1, tiled=True)
    cross = lax.dot_general(gp, hid, (((1,), (0,)), ((), ())), preferred_element_type=F32)
    later = jnp.arange(S) > k
    cross = jnp.where(later[:, None, None], cross, 0.0).astype(BF)
    cross = lax.psum(cross, "fsdp")
    far_in = dot(xs[1], small[1], 0, 0).astype(BF)
    far_in = lax.ppermute(far_in, "section", [(i, S - 1 - i) for i in range(S)])
    grad_in = dot(xs[0], small[0], 0, 0) + far_in.astype(F32)
    grad_out = dot(small[2:].reshape(2 * N, R), gs.reshape(2 * N, -1), 0, 0)
    grad_out = grad_out + lax.dot_general(
        cross, w_all, (((0, 1), (0, 2)), ((), ())), preferred_element_type=F32
    )
    return (grad_in[None], grad_out[None])


def solution(mesh):
    in_specs = (
        P("section", "fsdp", None),
        P("section", None, "fsdp"),
        P("section", None, "fsdp", None),
        P("section", None, "fsdp", None),
        P(None, None, "fsdp", None),
        P(),
        P(),
        P(),
        P(),
    )
    out_specs = (P("section", "fsdp", None), P("section", None, "fsdp"))
    return jax.shard_map(
        on_device, mesh=mesh, in_specs=in_specs, out_specs=out_specs, check_vma=False
    )
```

```python
import functools

import jax
import jax.numpy as jnp
from jax import lax
from jax.experimental import pallas as pl
from jax.experimental.pallas import tpu as pltpu
from jax.sharding import PartitionSpec as P

BF = jnp.bfloat16
F32 = jnp.float32
MESH = pl.DeviceIdType.MESH


def dot(a, b, ca, cb):
    return lax.dot_general(a, b, (((ca,), (cb,)), ((), ())), preferred_element_type=F32)


def kernel(
    S, F,
    xd_ref, xu_ref, win_ref, wout_ref, top_ref, roww_ref, head_ref, order_ref,
    gin_ref, gout_ref,
    xs, wo, wall, gf, gs, pp, pr, mp, mr, mt, farp, farr, gp, hid, smd, smu, cs, cr,
    gfar, gfr, acc, ds,
    s_loc, s_xs, s_xr, s_wos, s_wor, s_ws, s_wr, s_gs, s_gr, s_ps, s_pr, s_ms, s_mr,
    s_f, s_gps, s_gpr, s_hs, s_hr, s_ds, s_dr, s_us, s_ur, s_cs, s_cr, s_e,
):
    k = lax.axis_index("section")
    f = lax.axis_index("fsdp")
    mir = S - 1 - k
    n, R, Ds = xs.shape[2], wall.shape[2], wall.shape[1]
    Z = S // 2
    z, y = k // 2, k % 2

    def rc(src, dst, ss, rs, dev):
        return pltpu.make_async_remote_copy(
            src_ref=src, dst_ref=dst, send_sem=ss, recv_sem=rs, device_id=dev, device_id_type=MESH
        )

    peers = [lax.rem(f + j, F) for j in range(1, F)]

    barrier = pltpu.get_barrier_semaphore()
    for p in peers:
        pl.semaphore_signal(barrier, inc=1, device_id=(k, p), device_id_type=MESH)
    for j in range(1, S):
        pl.semaphore_signal(
            barrier, inc=1, device_id=(lax.rem(k + j, S), f), device_id_type=MESH
        )
    pl.semaphore_wait(barrier, S - 1 + F - 1)

    def cols(p):
        return pl.ds(pl.multiple_of(p * Ds, Ds), Ds)

    def x_copies(p, j):
        return [
            rc(xd_ref.at[:, cols(p)], xs.at[0, f], s_xs.at[0, j], s_xr.at[0, f], (k, p)),
            rc(xu_ref.at[:, cols(p)], xs.at[1, f], s_xs.at[1, j], s_xr.at[1, f], (k, p)),
        ]

    def wo_copy(p, j):
        return rc(wout_ref, wo.at[f], s_wos.at[j], s_wor.at[f], (k, p))

    def w_copy(src, s, way):
        dev = [(k + 2, f), (k - 2, f), (k + 1 - 2 * y, f)][way]
        return rc(src, wall.at[s], s_ws.at[s, way], s_wr.at[s], dev)

    local = [
        pltpu.make_async_copy(win_ref, wall.at[k], s_loc.at[0]),
        pltpu.make_async_copy(wout_ref, wo.at[f], s_loc.at[1]),
        pltpu.make_async_copy(xd_ref.at[:, cols(f)], xs.at[0, f], s_loc.at[2]),
        pltpu.make_async_copy(xu_ref.at[:, cols(f)], xs.at[1, f], s_loc.at[3]),
    ]

    @pl.when(z < Z - 1)
    def _():
        w_copy(win_ref, k, 0).start()

    @pl.when(z > 0)
    def _():
        w_copy(win_ref, k, 1).start()

    w_copy(win_ref, k, 2).start()
    for j, p in enumerate(peers):
        for c in x_copies(p, j):
            c.start()
    for c in local:
        c.start()
    for j, p in enumerate(peers):
        wo_copy(p, j).start()

    @pl.loop(0, F)
    def _(c):
        block = top_ref[:, cols(c)].astype(F32) + roww_ref[...] * head_ref[:, cols(c)]
        gf[c] = block.astype(BF)

    gs[f] = gf[f]

    for t in range(1, Z):
        lo, hi = k - 2 * t, k + 2 * t

        @pl.when(z - t >= 0)
        def _():
            w_copy(wall.at[lo], lo, 0).wait_recv()

            @pl.when(z < Z - 1)
            def _():
                w_copy(wall.at[lo], lo, 0).start()

            w_copy(wall.at[lo], lo, 2).start()

        @pl.when(z + t < Z)
        def _():
            w_copy(wall.at[hi], hi, 1).wait_recv()

            @pl.when(z > 0)
            def _():
                w_copy(wall.at[hi], hi, 1).start()

            w_copy(wall.at[hi], hi, 2).start()

    for c in local:
        c.wait()

    @pl.loop(0, Z)
    def _(t):
        s = 2 * t + 1 - y
        w_copy(wall.at[s], s, 2).wait_recv()

    def pp_copy(p, j):
        return rc(pp.at[p], pr.at[f], s_ps.at[j], s_pr.at[f], (k, p))

    def pre_part(p):
        a = dot(xs[0, p], wall[k], 1, 0)
        b = dot(xs[1, p], wall[mir], 1, 0)
        pp[p, 0] = a.astype(BF)
        pp[p, 1] = b.astype(BF)

    def m_copy(p, j):
        return rc(mp, mr.at[f], s_ms.at[j], s_mr.at[f], (k, p))

    @pl.loop(0, S)
    def _(s):
        mp[s] = dot(wout_ref[...], wall[s], 1, 0).astype(BF)

    for j, p in enumerate(peers):
        m_copy(p, j).start()
    pre_part(f)

    @pl.loop(1, F)
    def _(j):
        p = lax.rem(f + j, F)
        rc(xs.at[0, p], xs.at[0, p], s_xs.at[0, 0], s_xr.at[0, p], (k, p)).wait_recv()
        rc(xs.at[1, p], xs.at[1, p], s_xs.at[1, 0], s_xr.at[1, p], (k, p)).wait_recv()
        pre_part(p)
        pp_copy(p, j - 1).start()

    acc[...] = dot(gf[f], wo[f], 1, 1)

    @pl.loop(1, F)
    def _(j):
        p = lax.rem(f + j, F)
        rc(wo.at[p], wo.at[p], s_wos.at[0], s_wor.at[p], (k, p)).wait_recv()
        acc[...] += dot(gf[p], wo[p], 1, 1)

    pd = pp[f, 0].astype(F32)
    pu = pp[f, 1].astype(F32)
    for p in peers:
        rc(pr.at[p], pr.at[p], s_ps.at[0], s_pr.at[p], (k, p)).wait_recv()
        pd = pd + pr[p, 0].astype(F32)
        pu = pu + pr[p, 1].astype(F32)
    farp[...] = dot(order_ref[1], pu.astype(BF), 1, 0).astype(BF)
    far_copy = rc(farp, farr, s_f.at[0], s_f.at[1], (mir, f))
    far_copy.start()

    def g_copy(p, j):
        return rc(gf.at[p], gs.at[f], s_gs.at[j], s_gr.at[f], (k, p))

    for j, p in enumerate(peers):
        g_copy(p, j).start()

    def gate(rows, pre):
        sig = jax.nn.sigmoid(pre)
        hid[f, rows] = (pre * sig).astype(BF)
        ds[rows] = sig * (1.0 + pre * (1.0 - sig))

    gate(pl.ds(0, n), dot(order_ref[0], pd.astype(BF), 1, 0))

    for p in peers:
        rc(mr.at[p], mr.at[p], s_ms.at[0], s_mr.at[p], (k, p)).wait_recv()

    @pl.loop(0, S)
    def _(s):
        total = mp[s].astype(F32)
        for p in peers:
            total = total + mr[p, s].astype(F32)
        mt[s] = total.astype(BF)

    far_copy.wait_recv()
    gate(pl.ds(n, n), farr[...].astype(F32))

    def h_copy(p, j):
        return rc(hid.at[f], hid.at[f], s_hs.at[j], s_hr.at[f], (k, p))

    for j, p in enumerate(peers):
        h_copy(p, j).start()

    def gp_copy(to):
        return rc(gp.at[k], gp.at[k], s_gps.at[to], s_gpr.at[k], (to, f))

    def gp_arrived(s):
        rc(gp.at[s], gp.at[s], s_gps.at[0], s_gpr.at[s], (s, f)).wait_recv()

    def finish():
        gp[k] = (acc[...] * ds[...]).astype(BF)

        @pl.loop(0, k)
        def _(i):
            gp_copy(k - 1 - i).start()

        @pl.when(mir > k)
        def _():
            gp_copy(mir).start()

    def c_copy(s, p, j):
        return rc(cs.at[s], cr.at[f, s], s_cs.at[s, j], s_cr.at[f, s], (k, p))

    @pl.when(k == S - 1)
    def _():
        finish()

    @pl.loop(0, S - 1 - k)
    def _(i):
        s = S - 1 - i
        gp_arrived(s)
        acc[...] += dot(gp[s], mt[s], 1, 1)

        @pl.when(s == k + 1)
        def _():
            finish()

        cs[s] = dot(hid[f], gp[s], 0, 0).astype(BF)
        for j, p in enumerate(peers):
            c_copy(s, p, j).start()

    def d_copy(p, j):
        return rc(smd.at[f], smd.at[f], s_ds.at[j], s_dr.at[f], (k, p))

    def u_copy(p, j):
        return rc(smu.at[f], smu.at[f], s_us.at[j], s_ur.at[f], (k, p))

    smd[f] = dot(order_ref[0], gp[k, pl.ds(0, n)], 0, 0).astype(BF)
    for j, p in enumerate(peers):
        d_copy(p, j).start()

    @pl.when(mir < k)
    def _():
        gp_arrived(mir)

    smu[f] = dot(order_ref[1], gp[mir, pl.ds(n, n)], 0, 0).astype(BF)
    for j, p in enumerate(peers):
        u_copy(p, j).start()
    for p in peers:
        rc(smu.at[p], smu.at[p], s_us.at[0], s_ur.at[p], (k, p)).wait_recv()
        rc(smd.at[p], smd.at[p], s_ds.at[0], s_dr.at[p], (k, p)).wait_recv()

    gin_ref[...] = dot(xs[1, 0], smu[0], 0, 0)

    @pl.loop(1, F)
    def _(c):
        gin_ref[...] += dot(xs[1, c], smu[c], 0, 0)

    gfar[...] = gin_ref[...].astype(BF)
    e_copy = rc(gfar, gfr, s_e.at[0], s_e.at[1], (mir, f))
    e_copy.start()

    gin_ref[...] = dot(xs[0, 0], smd[0], 0, 0)

    @pl.loop(1, F)
    def _(c):
        gin_ref[...] += dot(xs[0, c], smd[c], 0, 0)

    gout_ref[...] = dot(hid[f], gs[f], 0, 0)

    @pl.loop(1, F)
    def _(j):
        p = lax.rem(f + j, F)
        rc(hid.at[p], hid.at[p], s_hs.at[0], s_hr.at[p], (k, p)).wait_recv()
        rc(gs.at[p], gs.at[p], s_gs.at[0], s_gr.at[p], (k, p)).wait_recv()
        gout_ref[...] += dot(hid[p], gs[p], 0, 0)

    @pl.loop(0, S - 1 - k)
    def _(i):
        s = S - 1 - i
        total = cs[s].astype(F32)
        for p in peers:
            rc(cr.at[p, s], cr.at[p, s], s_cs.at[s, 0], s_cr.at[p, s], (k, p)).wait_recv()
            total = total + cr[p, s].astype(F32)
        gout_ref[...] += dot(total.astype(BF), wall[s], 1, 1)

    e_copy.wait_recv()
    gin_ref[...] += gfr[...].astype(F32)

    for j, p in enumerate(peers):
        for c in x_copies(p, j):
            c.wait_send()
        for c in (wo_copy, m_copy, pp_copy, g_copy, h_copy, d_copy, u_copy):
            c(p, j).wait_send()

    @pl.loop(0, S - 1 - k)
    def _(i):
        s = S - 1 - i
        for j, p in enumerate(peers):
            c_copy(s, p, j).wait_send()

    far_copy.wait_send()
    e_copy.wait_send()

    @pl.loop(0, k)
    def _(i):
        gp_copy(i).wait_send()

    @pl.when(mir > k)
    def _():
        gp_copy(mir).wait_send()

    for t in range(0, Z):
        lo, hi = k - 2 * t, k + 2 * t

        @pl.when(z - t >= 0)
        def _():
            @pl.when(z < Z - 1)
            def _():
                w_copy(wall.at[lo], lo, 0).wait_send()

            w_copy(wall.at[lo], lo, 2).wait_send()

        if t > 0:

            @pl.when(z + t < Z)
            def _():
                @pl.when(z > 0)
                def _():
                    w_copy(wall.at[hi], hi, 1).wait_send()

                w_copy(wall.at[hi], hi, 2).wait_send()

        else:

            @pl.when(z > 0)
            def _():
                w_copy(wall.at[hi], hi, 1).wait_send()


def on_device(
    branch_in,
    branch_out,
    down_inputs,
    up_inputs,
    top_grads,
    plan,
    reward_pos,
    reward_cot,
    reward_head,
):
    S = lax.axis_size("section")
    F = lax.axis_size("fsdp")
    f = lax.axis_index("fsdp")
    _, micro, r, D = down_inputs.shape
    n = micro * r
    seqs = reward_pos.shape[2]
    seq_len = r * F // seqs
    w_in, w_out = branch_in[0], branch_out[0]
    Ds, R = w_in.shape

    row_global = f * r + jnp.arange(r, dtype=jnp.int32)
    pick = plan[:, :, None] == jnp.arange(micro, dtype=jnp.int32)
    pos = jnp.sum(jnp.where(pick[..., None], reward_pos[:, None], 0), axis=2)
    cot = jnp.sum(jnp.where(pick[..., None], reward_cot[:, None], 0.0), axis=2)
    target = jnp.arange(seqs, dtype=jnp.int32) * seq_len + pos
    weight = jnp.sum(jnp.where(target[..., None] == row_global, cot[..., None], 0.0), axis=2)
    row = jnp.arange(n, dtype=jnp.int32)
    match = jnp.repeat(plan, r, axis=1) * r + row % r
    order = (match[:, :, None] == row).astype(BF)

    vm = pltpu.VMEM
    dma = pltpu.SemaphoreType.DMA
    anyspec = pl.BlockSpec(memory_space=pl.ANY)
    vspec = pl.BlockSpec(memory_space=pltpu.VMEM)
    gin, gout = pl.pallas_call(
        functools.partial(kernel, S, F),
        out_shape=(
            jax.ShapeDtypeStruct((Ds, R), F32),
            jax.ShapeDtypeStruct((R, Ds), F32),
        ),
        in_specs=[anyspec, anyspec, vspec, vspec, vspec, vspec, vspec, vspec],
        out_specs=(vspec, vspec),
        scratch_shapes=[
            vm((2, F, n, Ds), BF),
            vm((F, R, Ds), BF),
            vm((S, Ds, R), BF),
            vm((F, 2 * n, Ds), BF),
            vm((F, 2 * n, Ds), BF),
            vm((F, 2, n, R), BF),
            vm((F, 2, n, R), BF),
            vm((S, R, R), BF),
            vm((F, S, R, R), BF),
            vm((S, R, R), BF),
            vm((n, R), BF),
            vm((n, R), BF),
            vm((S, 2 * n, R), BF),
            vm((F, 2 * n, R), BF),
            vm((F, n, R), BF),
            vm((F, n, R), BF),
            vm((S, R, R), BF),
            vm((F, S, R, R), BF),
            vm((Ds, R), BF),
            vm((Ds, R), BF),
            vm((2 * n, R), F32),
            vm((2 * n, R), F32),
            dma((4,)),
            dma((2, F)), dma((2, F)),
            dma((F,)), dma((F,)),
            dma((S, 3)), dma((S,)),
            dma((F,)), dma((F,)),
            dma((F,)), dma((F,)),
            dma((F,)), dma((F,)),
            dma((2,)),
            dma((S,)), dma((S,)),
            dma((F,)), dma((F,)),
            dma((F,)), dma((F,)),
            dma((F,)), dma((F,)),
            dma((S, F)), dma((F, S)),
            dma((2,)),
        ],
        compiler_params=pltpu.CompilerParams(
            collective_id=0, has_side_effects=True, vmem_limit_bytes=54 * 2**20
        ),
        cost_estimate=pl.CostEstimate(
            flops=16 * F * n * Ds * R, bytes_accessed=16 * n * D, transcendentals=2 * n * R
        ),
    )(
        down_inputs.reshape(n, D),
        up_inputs.reshape(n, D),
        w_in,
        w_out,
        top_grads.reshape(2 * n, D),
        weight.reshape(2 * n, 1),
        reward_head.reshape(1, D),
        order,
    )
    return (gin[None], gout[None])


def solution(mesh):
    in_specs = (
        P("section", "fsdp", None),
        P("section", None, "fsdp"),
        P("section", None, "fsdp", None),
        P("section", None, "fsdp", None),
        P(None, None, "fsdp", None),
        P(),
        P(),
        P(),
        P(),
    )
    out_specs = (P("section", "fsdp", None), P("section", None, "fsdp"))
    return jax.shard_map(
        on_device, mesh=mesh, in_specs=in_specs, out_specs=out_specs, check_vma=False
    )
```

```python
import functools

import jax
import jax.numpy as jnp
from jax import lax
from jax.experimental import pallas as pl
from jax.experimental.pallas import tpu as pltpu
from jax.sharding import PartitionSpec as P

BF = jnp.bfloat16
F32 = jnp.float32
MESH = pl.DeviceIdType.MESH


def dot(a, b, ca, cb):
    return lax.dot_general(a, b, (((ca,), (cb,)), ((), ())), preferred_element_type=F32)


def kernel(
    S, F,
    xd_ref, xu_ref, win_ref, wout_ref, top_ref, roww_ref, head_ref, order_ref,
    gin_ref, gout_ref,
    xs, wo, wall, gf, gs, pp, pr, mp, mr, mt, farp, farr, gp, hid, smd, smu, cs, cr,
    gfar, gfr, acc, ds,
    s_loc, s_xs, s_xr, s_wos, s_wof, s_wor, s_ws, s_wr, s_gs, s_gf, s_gr, s_ps, s_pr, s_ms, s_mr,
    s_f, s_gps, s_gpr, s_hs, s_hr, s_ds, s_dr, s_us, s_ur, s_cs, s_cr, s_e,
):
    k = lax.axis_index("section")
    f = lax.axis_index("fsdp")
    mir = S - 1 - k
    n, R, Ds = xs.shape[2], wall.shape[2], wall.shape[1]
    Z = S // 2
    z, y = k // 2, k % 2

    def rc(src, dst, ss, rs, dev):
        return pltpu.make_async_remote_copy(
            src_ref=src, dst_ref=dst, send_sem=ss, recv_sem=rs, device_id=dev, device_id_type=MESH
        )

    core, chips = f % 2, F // 2
    sib, across = f + 1 - 2 * core, k + 1 - 2 * y
    peers = [sib]
    for j in range(1, chips):
        chip = lax.rem(f // 2 + j, chips)
        peers += [2 * chip + core, 2 * chip + 1 - core]
    same = list(range(1, F - 1, 2))

    barrier = pltpu.get_barrier_semaphore()
    for p in peers:
        pl.semaphore_signal(barrier, inc=1, device_id=(k, p), device_id_type=MESH)
    for j in range(1, S):
        pl.semaphore_signal(
            barrier, inc=1, device_id=(lax.rem(k + j, S), f), device_id_type=MESH
        )
    pl.semaphore_wait(barrier, S - 1 + F - 1)

    def cols(p):
        return pl.ds(pl.multiple_of(p * Ds, Ds), Ds)

    def x_copies(p, j):
        return [
            rc(xd_ref.at[:, cols(p)], xs.at[0, f], s_xs.at[0, j], s_xr.at[0, f], (k, p)),
            rc(xu_ref.at[:, cols(p)], xs.at[1, f], s_xs.at[1, j], s_xr.at[1, f], (k, p)),
        ]

    def wo_copy(p, j):
        return rc(wout_ref, wo.at[f], s_wos.at[j], s_wor.at[f], (k, p))

    def w_copy(src, s, way):
        dev = [(k + 2, f), (k - 2, f), (k + 1 - 2 * y, f)][way]
        return rc(src, wall.at[s], s_ws.at[s, way], s_wr.at[s], dev)

    local = [
        pltpu.make_async_copy(win_ref, wall.at[k], s_loc.at[0]),
        pltpu.make_async_copy(wout_ref, wo.at[f], s_loc.at[1]),
        pltpu.make_async_copy(xd_ref.at[:, cols(f)], xs.at[0, f], s_loc.at[2]),
        pltpu.make_async_copy(xu_ref.at[:, cols(f)], xs.at[1, f], s_loc.at[3]),
    ]

    @pl.when(z < Z - 1)
    def _():
        w_copy(win_ref, k, 0).start()

    @pl.when(z > 0)
    def _():
        w_copy(win_ref, k, 1).start()

    w_copy(win_ref, k, 2).start()
    for j, p in enumerate(peers):
        for c in x_copies(p, j):
            c.start()
    for c in local:
        c.start()
    for j in [0] + same:
        wo_copy(peers[j], j).start()

    @pl.loop(0, F)
    def _(c):
        block = top_ref[:, cols(c)].astype(F32) + roww_ref[...] * head_ref[:, cols(c)]
        gf[c] = block.astype(BF)

    gs[f] = gf[f]

    for t in range(1, Z):
        lo, hi = k - 2 * t, k + 2 * t

        @pl.when(z - t >= 0)
        def _():
            w_copy(wall.at[lo], lo, 0).wait_recv()

            @pl.when(z < Z - 1)
            def _():
                w_copy(wall.at[lo], lo, 0).start()

            w_copy(wall.at[lo], lo, 2).start()

        @pl.when(z + t < Z)
        def _():
            w_copy(wall.at[hi], hi, 1).wait_recv()

            @pl.when(z > 0)
            def _():
                w_copy(wall.at[hi], hi, 1).start()

            w_copy(wall.at[hi], hi, 2).start()

    for c in local:
        c.wait()

    @pl.loop(0, Z)
    def _(t):
        s = 2 * t + 1 - y
        w_copy(wall.at[s], s, 2).wait_recv()

    def pp_copy(p, j):
        return rc(pp.at[p], pr.at[f], s_ps.at[p], s_pr.at[f], (k, p))

    def pre_part(p):
        a = dot(xs[0, p], wall[k], 1, 0)
        b = dot(xs[1, p], wall[mir], 1, 0)
        pp[p, 0] = a.astype(BF)
        pp[p, 1] = b.astype(BF)

    pre_part(f)

    @pl.loop(1, F)
    def _(j):
        p = lax.rem(f + j, F)
        rc(xs.at[0, p], xs.at[0, p], s_xs.at[0, 0], s_xr.at[0, p], (k, p)).wait_recv()
        rc(xs.at[1, p], xs.at[1, p], s_xs.at[1, 0], s_xr.at[1, p], (k, p)).wait_recv()
        pre_part(p)
        pp_copy(p, j - 1).start()

    def wo_pass(j):
        p = peers[j]
        return rc(wo.at[p], wo.at[p], s_wof.at[j], s_wor.at[p], (k, sib))

    for j in same:
        p = peers[j]
        rc(wo.at[p], wo.at[p], s_wos.at[0], s_wor.at[p], (k, p)).wait_recv()
        wo_pass(j).start()

    def rows(d):
        return pl.ds(pl.multiple_of(d * n, 16), n)

    def g_copy(p, j):
        return rc(gf.at[p, rows(y)], gs.at[f, rows(y)], s_gs.at[j], s_gr.at[y, f], (k, p))

    g_sib = rc(
        gf.at[sib, rows(1 - y)], gs.at[f, rows(1 - y)], s_gs.at[F - 1], s_gr.at[1 - y, f], (k, sib)
    )

    def g_pass(j):
        p = peers[j]
        return rc(
            gs.at[p, rows(y)], gs.at[p, rows(y)], s_gf.at[j], s_gr.at[y, p], (across, f)
        )

    for j, p in enumerate(peers):
        g_copy(p, j).start()
    g_sib.start()

    acc[...] = dot(gf[f], wo[f], 1, 1)

    @pl.loop(1, F)
    def _(j):
        p = lax.rem(f + j, F)

        @pl.when(jnp.logical_or(p == sib, p % 2 != core))
        def _():
            rc(wo.at[p], wo.at[p], s_wos.at[0], s_wor.at[p], (k, p)).wait_recv()

        acc[...] += dot(gf[p], wo[p], 1, 1)

    pd = pp[f, 0].astype(F32)
    pu = pp[f, 1].astype(F32)
    for p in peers:
        rc(pr.at[p], pr.at[p], s_ps.at[0], s_pr.at[p], (k, p)).wait_recv()
        pd = pd + pr[p, 0].astype(F32)
        pu = pu + pr[p, 1].astype(F32)
    farp[...] = dot(order_ref[1], pu.astype(BF), 1, 0).astype(BF)
    far_copy = rc(farp, farr, s_f.at[0], s_f.at[1], (mir, f))
    far_copy.start()

    def gate(at, pre):
        sig = jax.nn.sigmoid(pre)
        hid[f, at] = (pre * sig).astype(BF)
        ds[at] = sig * (1.0 + pre * (1.0 - sig))

    gate(pl.ds(0, n), dot(order_ref[0], pd.astype(BF), 1, 0))

    def m_copy(s, p, j):
        return rc(mp.at[s], mr.at[f, s], s_ms.at[s, j], s_mr.at[f, s], (k, p))

    @pl.loop(0, S - 1 - k)
    def _(i):
        s = S - 1 - i
        mp[s] = dot(wout_ref[...], wall[s], 1, 0).astype(BF)
        for j, p in enumerate(peers):
            m_copy(s, p, j).start()

    far_copy.wait_recv()
    gate(pl.ds(n, n), farr[...].astype(F32))

    def h_copy(p, j):
        return rc(hid.at[f], hid.at[f], s_hs.at[j], s_hr.at[f], (k, p))

    for j, p in enumerate(peers):
        h_copy(p, j).start()

    for j in range(1, F - 1):
        p = peers[j]
        g_pass(j).wait_recv()
        g_pass(j).start()

    def gp_copy(to):
        return rc(gp.at[k], gp.at[k], s_gps.at[to], s_gpr.at[k], (to, f))

    def gp_arrived(s):
        rc(gp.at[s], gp.at[s], s_gps.at[0], s_gpr.at[s], (s, f)).wait_recv()

    def finish():
        gp[k] = (acc[...] * ds[...]).astype(BF)

        @pl.loop(0, k)
        def _(i):
            gp_copy(k - 1 - i).start()

        @pl.when(mir > k)
        def _():
            gp_copy(mir).start()

    def c_copy(s, p, j):
        return rc(cs.at[s], cr.at[f, s], s_cs.at[s, j], s_cr.at[f, s], (k, p))

    @pl.when(k == S - 1)
    def _():
        finish()

    @pl.loop(0, S - 1 - k)
    def _(i):
        s = S - 1 - i
        total = mp[s].astype(F32)
        for p in peers:
            rc(mr.at[p, s], mr.at[p, s], s_ms.at[s, 0], s_mr.at[p, s], (k, p)).wait_recv()
            total = total + mr[p, s].astype(F32)
        mt[...] = total.astype(BF)
        gp_arrived(s)
        acc[...] += dot(gp[s], mt[...], 1, 1)

        @pl.when(s == k + 1)
        def _():
            finish()

        cs[s] = dot(hid[f], gp[s], 0, 0).astype(BF)
        for j, p in enumerate(peers):
            c_copy(s, p, j).start()

    def d_copy(p, j):
        return rc(smd.at[f], smd.at[f], s_ds.at[j], s_dr.at[f], (k, p))

    def u_copy(p, j):
        return rc(smu.at[f], smu.at[f], s_us.at[j], s_ur.at[f], (k, p))

    smd[f] = dot(order_ref[0], gp[k, pl.ds(0, n)], 0, 0).astype(BF)
    for j, p in enumerate(peers):
        d_copy(p, j).start()

    @pl.when(mir < k)
    def _():
        gp_arrived(mir)

    smu[f] = dot(order_ref[1], gp[mir, pl.ds(n, n)], 0, 0).astype(BF)
    for j, p in enumerate(peers):
        u_copy(p, j).start()
    for p in peers:
        rc(smu.at[p], smu.at[p], s_us.at[0], s_ur.at[p], (k, p)).wait_recv()
        rc(smd.at[p], smd.at[p], s_ds.at[0], s_dr.at[p], (k, p)).wait_recv()

    gin_ref[...] = dot(xs[1, 0], smu[0], 0, 0)

    @pl.loop(1, F)
    def _(c):
        gin_ref[...] += dot(xs[1, c], smu[c], 0, 0)

    gfar[...] = gin_ref[...].astype(BF)
    e_copy = rc(gfar, gfr, s_e.at[0], s_e.at[1], (mir, f))
    e_copy.start()

    gin_ref[...] = dot(xs[0, 0], smd[0], 0, 0)

    @pl.loop(1, F)
    def _(c):
        gin_ref[...] += dot(xs[0, c], smd[c], 0, 0)

    gout_ref[...] = dot(hid[f], gs[f], 0, 0)

    @pl.loop(1, F)
    def _(j):
        p = lax.rem(f + j, F)
        rc(hid.at[p], hid.at[p], s_hs.at[0], s_hr.at[p], (k, p)).wait_recv()

        @pl.when(p == sib)
        def _():
            rc(
                gs.at[p, rows(y)], gs.at[p, rows(y)], s_gs.at[0], s_gr.at[y, p], (k, p)
            ).wait_recv()

        rc(
            gs.at[p, rows(1 - y)], gs.at[p, rows(1 - y)], s_gs.at[0], s_gr.at[1 - y, p], (k, p)
        ).wait_recv()
        gout_ref[...] += dot(hid[p], gs[p], 0, 0)

    @pl.loop(0, S - 1 - k)
    def _(i):
        s = S - 1 - i
        total = cs[s].astype(F32)
        for p in peers:
            rc(cr.at[p, s], cr.at[p, s], s_cs.at[s, 0], s_cr.at[p, s], (k, p)).wait_recv()
            total = total + cr[p, s].astype(F32)
        gout_ref[...] += dot(total.astype(BF), wall[s], 1, 1)

    e_copy.wait_recv()
    gin_ref[...] += gfr[...].astype(F32)

    for j, p in enumerate(peers):
        for c in x_copies(p, j):
            c.wait_send()
        for c in (pp_copy, g_copy, h_copy, d_copy, u_copy):
            c(p, j).wait_send()
    g_sib.wait_send()
    for j in [0] + same:
        wo_copy(peers[j], j).wait_send()
    for j in same:
        wo_pass(j).wait_send()
    for j in range(1, F - 1):
        g_pass(j).wait_send()

    @pl.loop(0, S - 1 - k)
    def _(i):
        s = S - 1 - i
        for j, p in enumerate(peers):
            c_copy(s, p, j).wait_send()
            m_copy(s, p, j).wait_send()

    far_copy.wait_send()
    e_copy.wait_send()

    @pl.loop(0, k)
    def _(i):
        gp_copy(i).wait_send()

    @pl.when(mir > k)
    def _():
        gp_copy(mir).wait_send()

    for t in range(0, Z):
        lo, hi = k - 2 * t, k + 2 * t

        @pl.when(z - t >= 0)
        def _():
            @pl.when(z < Z - 1)
            def _():
                w_copy(wall.at[lo], lo, 0).wait_send()

            w_copy(wall.at[lo], lo, 2).wait_send()

        if t > 0:

            @pl.when(z + t < Z)
            def _():
                @pl.when(z > 0)
                def _():
                    w_copy(wall.at[hi], hi, 1).wait_send()

                w_copy(wall.at[hi], hi, 2).wait_send()

        else:

            @pl.when(z > 0)
            def _():
                w_copy(wall.at[hi], hi, 1).wait_send()


def on_device(
    branch_in,
    branch_out,
    down_inputs,
    up_inputs,
    top_grads,
    plan,
    reward_pos,
    reward_cot,
    reward_head,
):
    S = lax.axis_size("section")
    F = lax.axis_size("fsdp")
    f = lax.axis_index("fsdp")
    _, micro, r, D = down_inputs.shape
    n = micro * r
    seqs = reward_pos.shape[2]
    seq_len = r * F // seqs
    w_in, w_out = branch_in[0], branch_out[0]
    Ds, R = w_in.shape

    row_global = f * r + jnp.arange(r, dtype=jnp.int32)
    pick = plan[:, :, None] == jnp.arange(micro, dtype=jnp.int32)
    pos = jnp.sum(jnp.where(pick[..., None], reward_pos[:, None], 0), axis=2)
    cot = jnp.sum(jnp.where(pick[..., None], reward_cot[:, None], 0.0), axis=2)
    target = jnp.arange(seqs, dtype=jnp.int32) * seq_len + pos
    weight = jnp.sum(jnp.where(target[..., None] == row_global, cot[..., None], 0.0), axis=2)
    row = jnp.arange(n, dtype=jnp.int32)
    match = jnp.repeat(plan, r, axis=1) * r + row % r
    order = (match[:, :, None] == row).astype(BF)

    vm = pltpu.VMEM
    dma = pltpu.SemaphoreType.DMA
    anyspec = pl.BlockSpec(memory_space=pl.ANY)
    vspec = pl.BlockSpec(memory_space=pltpu.VMEM)
    gin, gout = pl.pallas_call(
        functools.partial(kernel, S, F),
        out_shape=(
            jax.ShapeDtypeStruct((Ds, R), F32),
            jax.ShapeDtypeStruct((R, Ds), F32),
        ),
        in_specs=[anyspec, anyspec, vspec, vspec, vspec, vspec, vspec, vspec],
        out_specs=(vspec, vspec),
        scratch_shapes=[
            vm((2, F, n, Ds), BF),
            vm((F, R, Ds), BF),
            vm((S, Ds, R), BF),
            vm((F, 2 * n, Ds), BF),
            vm((F, 2 * n, Ds), BF),
            vm((F, 2, n, R), BF),
            vm((F, 2, n, R), BF),
            vm((S, R, R), BF),
            vm((F, S, R, R), BF),
            vm((R, R), BF),
            vm((n, R), BF),
            vm((n, R), BF),
            vm((S, 2 * n, R), BF),
            vm((F, 2 * n, R), BF),
            vm((F, n, R), BF),
            vm((F, n, R), BF),
            vm((S, R, R), BF),
            vm((F, S, R, R), BF),
            vm((Ds, R), BF),
            vm((Ds, R), BF),
            vm((2 * n, R), F32),
            vm((2 * n, R), F32),
            dma((4,)),
            dma((2, F)), dma((2, F)),
            dma((F,)), dma((F,)), dma((F,)),
            dma((S, 3)), dma((S,)),
            dma((F,)), dma((F,)), dma((2, F)),
            dma((F,)), dma((F,)),
            dma((S, F)), dma((F, S)),
            dma((2,)),
            dma((S,)), dma((S,)),
            dma((F,)), dma((F,)),
            dma((F,)), dma((F,)),
            dma((F,)), dma((F,)),
            dma((S, F)), dma((F, S)),
            dma((2,)),
        ],
        compiler_params=pltpu.CompilerParams(
            collective_id=0, has_side_effects=True, vmem_limit_bytes=54 * 2**20
        ),
        cost_estimate=pl.CostEstimate(
            flops=16 * F * n * Ds * R, bytes_accessed=16 * n * D, transcendentals=2 * n * R
        ),
    )(
        down_inputs.reshape(n, D),
        up_inputs.reshape(n, D),
        w_in,
        w_out,
        top_grads.reshape(2 * n, D),
        weight.reshape(2 * n, 1),
        reward_head.reshape(1, D),
        order,
    )
    return (gin[None], gout[None])


def solution(mesh):
    in_specs = (
        P("section", "fsdp", None),
        P("section", None, "fsdp"),
        P("section", None, "fsdp", None),
        P("section", None, "fsdp", None),
        P(None, None, "fsdp", None),
        P(),
        P(),
        P(),
        P(),
    )
    out_specs = (P("section", "fsdp", None), P("section", None, "fsdp"))
    return jax.shard_map(
        on_device, mesh=mesh, in_specs=in_specs, out_specs=out_specs, check_vma=False
    )
```
